32 devices in a mesh: seq: 16 (over z, y, x), dp: 2 (over core).
Axes of the slice: x: 2, y: 2, z: 4, core: 2. Of those that a mesh axis runs over, the one named last changes fastest.
Arguments:
- queries: bfloat16 [4, 1024, 4096], P('dp', 'seq'), may hold values from -300 to 300
- key_states: bfloat16 [4, 1024, 4096], P('dp', 'seq'), may hold values from -4.5 to 4.5
- value_states: bfloat16 [4, 1024, 4096], P('dp', 'seq'), may hold values from -6 to 6
- grad_output: bfloat16 [4, 1024, 4096], P('dp', 'seq'), may hold values from -6 to 6
- query_bias: bfloat16 [4096], P(('seq', 'dp')), may hold values from -5 to 5
Outputs:
- grad_queries: bfloat16 [4, 1024, 4096], P('dp', 'seq')
- grad_keys: bfloat16 [4, 1024, 4096], P('dp', 'seq')
- grad_values: bfloat16 [4, 1024, 4096], P('dp', 'seq')
- grad_bias: float32 [4096], P(('seq', 'dp'))
The draws below stay inside these ranges and needn't reach their ends.
All inputs are finite; a program needn't handle non-finite values.
Results may differ from the reference program's by a relative error of at most 0.007.
Values may be sent and summed in bfloat16 or wider, within the bound.
A program may use at most 128 MiB of HBM per device.

```python
import math
import jax
import jax.numpy as jnp
from jax import lax

HDIM = 128
QBLOCKS = 4
WIDTH = 4096
SEQ_LEN = 1024
SEQS = 4


def key_values(key):
    base_values = jax.random.normal(jax.random.fold_in(key, 11), (SEQS, SEQ_LEN, WIDTH), jnp.float32)
    base_values = jnp.clip(base_values, -4.5, 4.5)
    return base_values


def draw_key_states(key, part):
    return key_values(key).astype(jnp.bfloat16)


def draw_queries(key, part):
    base_values = jax.random.normal(jax.random.fold_in(key, 21), (SEQS, SEQ_LEN, WIDTH), jnp.float32)
    base_values = jnp.clip(base_values, -4.5, 4.5)
    return base_values.astype(jnp.bfloat16)


def block_levels(rng, shape, pieces, smallest, top_value):
    level, own = 1.0, jax.random.fold_in(rng, 6)
    for axis_at, shards_of in pieces:
        steps = jnp.exp(jax.random.uniform(jax.random.fold_in(own, axis_at), (shards_of,), jnp.float32, smallest / len(pieces), top_value / len(pieces)))
        level = level * jnp.repeat(steps, shape[axis_at] // shards_of).reshape([-1 if axis == axis_at else 1 for axis in range(len(shape))])
    return level


def noise(rng, shape, width, bound, cuts=(), kind=jnp.bfloat16):
    values = jax.random.normal(rng, shape, jnp.float32) * width
    if len(cuts) > 0:
        values = block_levels(rng, shape, cuts, -0.22, 0.18) * values
    return jnp.clip(values, min=-bound, max=bound).astype(kind)


def setup_inputs(seed: int = 0) -> dict:
    keys = jax.random.split(jax.random.key(seed), 6)
    queries = draw_queries(jax.random.fold_in(keys[5], 71), 0)
    key_states = draw_key_states(jax.random.fold_in(keys[5], 71), 0)
    value_states = noise(keys[2], (SEQS, SEQ_LEN, WIDTH), 1.0, 6.0, ((0, 2), (1, 16)))
    grad_output = noise(keys[3], (SEQS, SEQ_LEN, WIDTH), 1.0, 6.0, ((0, 2), (1, 16)))
    query_bias = noise(keys[4], (WIDTH,), 1.0, 5.0, ((0, 32),))
    return {"queries": queries, "key_states": key_states, "value_states": value_states, "grad_output": grad_output, "query_bias": query_bias}


masked_value = -1e+30

def attend(query_full, key_rows, value_rows, grad_rows):
    item_count, seq_length, total_cols = query_full.shape
    head_count = total_cols // HDIM

    def heads_view(values):
        return values.astype(jnp.float32).reshape(item_count, seq_length, head_count, HDIM)
    query_heads = heads_view(query_full)
    key_heads = heads_view(key_rows)
    value_heads = heads_view(value_rows)
    grad_heads = heads_view(grad_rows)
    factor = 1.0 / math.sqrt(HDIM)
    block_rows = seq_length // QBLOCKS
    high = lax.Precision.HIGHEST
    grad_keys = jnp.zeros((item_count, seq_length, head_count, HDIM), jnp.float32)
    grad_values = jnp.zeros((item_count, seq_length, head_count, HDIM), jnp.float32)
    query_parts = []
    for block_idx in range(QBLOCKS):
        row_start = block_idx * block_rows
        key_end = row_start + block_rows
        block_query = query_heads[:, row_start:key_end]
        seen_keys = key_heads[:, :key_end]
        seen_values = value_heads[:, :key_end]
        block_grad = grad_heads[:, row_start:key_end]
        scores = jnp.einsum('nqhd,nkhd->nhqk', block_query, seen_keys, precision=high) * factor
        row_ids = row_start + jnp.arange(block_rows)[:, None]
        key_ids = jnp.arange(key_end)[None, :]
        scores = jnp.where(key_ids <= row_ids, scores, masked_value)
        highest = lax.optimization_barrier(jnp.max(scores, axis=-1, keepdims=True))
        shifted = jnp.exp(scores - highest)
        weights = shifted / lax.optimization_barrier(jnp.sum(shifted, axis=-1, keepdims=True))
        grad_probs = jnp.einsum('nqhd,nkhd->nhqk', block_grad, seen_values, precision=high)
        row_dot = lax.optimization_barrier(jnp.sum(weights * grad_probs, axis=-1, keepdims=True))
        grad_scores = (weights * (grad_probs - row_dot) * factor).astype(jnp.bfloat16).astype(jnp.float32)
        weights_low = weights.astype(jnp.bfloat16).astype(jnp.float32)
        grad_values = grad_values.at[:, :key_end].add(jnp.einsum('nhqk,nqhd->nkhd', weights_low, block_grad, precision=high))
        grad_keys = grad_keys.at[:, :key_end].add(jnp.einsum('nhqk,nqhd->nkhd', grad_scores, block_query, precision=high))
        query_parts.append(jnp.einsum('nhqk,nkhd->nqhd', grad_scores, seen_keys, precision=high))
    grad_queries = jnp.concatenate(query_parts, axis=1)
    shape_out = (item_count, seq_length, total_cols)
    return (grad_queries.reshape(shape_out), grad_keys.reshape(shape_out), grad_values.reshape(shape_out))

def reference(queries, key_states, value_states, grad_output, query_bias):
    query_full = (queries.astype(jnp.float32) + query_bias.astype(jnp.float32)[None, None, :]).astype(jnp.bfloat16)

    def one_sequence(items):
        query_one, key_one, value_one, grad_one = items
        grad_q, grad_k, grad_v = attend(query_one[None], key_one[None], value_one[None], grad_one[None])
        return (grad_q[0].astype(jnp.bfloat16), grad_k[0].astype(jnp.bfloat16), grad_v[0].astype(jnp.bfloat16), lax.optimization_barrier(jnp.sum(grad_q[0], axis=0)))
    grad_queries, grad_keys, grad_values, bias_terms = lax.map(one_sequence, (query_full, key_states, value_states, grad_output))
    grad_bias = lax.optimization_barrier(jnp.sum(bias_terms, axis=0))
    return (grad_queries, grad_keys, grad_values, grad_bias)
```

```python
import functools
import math

import jax
import jax.numpy as jnp
from jax import lax
from jax.experimental import pallas as pl
from jax.experimental.pallas import tpu as pltpu
from jax.sharding import PartitionSpec as P

HDIM = 128
ROWS = 256
FACTOR = 1.0 / math.sqrt(HDIM)
MESH = pl.DeviceIdType.MESH


def dot(a, b, dims):
    return lax.dot_general(a, b, (dims, ((), ())), preferred_element_type=jnp.float32)


def wait_bytes(ref, sem):
    pltpu.make_async_copy(ref, ref, sem).wait()


def kernel(
    n, chunk_heads, parts,
    q_hbm, k_hbm, v_hbm, g_hbm, bias_ref,
    dq_hbm, dk_hbm, dv_hbm, sums_ref,
    q_in, g_in, k_in, v_in,
    dq_out, dk_out, dv_out,
    k_low, v_low, k_high, v_high,
    k_acc, v_acc,
    in_recv, in_send, low_recv, low_send,
    out_recv, out_send, high_recv, high_send, last_sem,
):
    m = n // 2
    me = lax.axis_index("seq")
    upper = me >= m
    lower = me < m
    g = lax.rem(me, m)
    base = me - g
    items, rows, _ = q_hbm.shape
    half = m * rows
    cols = chunk_heads * HDIM
    own = parts * cols
    chunks = items * parts

    barrier = pltpu.get_barrier_semaphore()

    def greet(i, _):
        pl.semaphore_signal(
            barrier, inc=1, device_id={"seq": lax.rem(me + i, n)}, device_id_type=MESH
        )
        return 0

    lax.fori_loop(1, n, greet, 0)
    pl.semaphore_wait(barrier, n - 1)

    def column(owner, part):
        return pl.ds(pl.multiple_of(owner * own + part * cols, 128), cols)

    def remote(src, dst, send, recv, peer):
        pltpu.make_async_remote_copy(
            src_ref=src, dst_ref=dst, send_sem=send, recv_sem=recv,
            device_id={"seq": peer}, device_id_type=MESH,
        ).start()

    sources = (q_hbm, g_hbm, k_hbm, v_hbm)
    landing = (q_in, g_in, k_in, v_in)

    def send_inputs(c, _):
        item, part = c // parts, lax.rem(c, parts)
        mine = pl.ds(pl.multiple_of(g * rows, rows), rows)
        at = pl.ds(pl.multiple_of(me * rows, rows), rows)

        def place(a):
            return landing[a].at[c, mine if a < 2 else at]

        def step(i, _):
            shift = (m - 1) - i // 2 - lax.rem(i, 2) * (m // 2)
            to = lax.rem(g + shift, m)

            @pl.when(lower)
            def _():
                for a in (2, 3):
                    remote(
                        sources[a].at[item, :, column(to, part)], landing[a].at[c, at],
                        low_send.at[c, a - 2], low_recv.at[c, a - 2], m + to,
                    )

            @pl.when(shift > 0)
            def _():
                for a in (2, 3, 0, 1):
                    remote(
                        sources[a].at[item, :, column(to, part)], place(a),
                        in_send.at[c, a], in_recv.at[c, a], base + to,
                    )
            return 0

        lax.fori_loop(0, m, step, 0)
        for a in range(4):
            pltpu.make_async_copy(
                sources[a].at[item, :, column(g, part)], place(a), in_recv.at[c, a]
            ).start()
        return 0

    lax.fori_loop(0, chunks, send_inputs, 0)
    sums_ref[...] = jnp.zeros_like(sums_ref)

    def attend(c, part, h, offset):
        lane = pl.ds(h * HDIM, HDIM)
        total = offset + half
        k = k_in[c, :total, lane]
        v = v_in[c, :total, lane]
        k_turned = k.astype(jnp.float32).T.astype(jnp.bfloat16)
        bias = bias_ref[pl.ds(part * chunk_heads + h, 1), :]
        for block in reversed(range(half // ROWS)):
            q_rows = pl.ds(block * ROWS, ROWS)
            end = offset + (block + 1) * ROWS
            q = (q_in[c, q_rows, lane].astype(jnp.float32) + bias).astype(jnp.bfloat16)
            go = g_in[c, q_rows, lane]
            s = dot(k[:end], q, ((1,), (1,))) * FACTOR
            key_ids = lax.broadcasted_iota(jnp.int32, (ROWS, ROWS), 0)
            row_ids = lax.broadcasted_iota(jnp.int32, (ROWS, ROWS), 1)
            corner = jnp.where(key_ids <= row_ids, s[end - ROWS:], -1e30)
            s = corner if end == ROWS else jnp.concatenate([s[:end - ROWS], corner], axis=0)
            e = jnp.exp(s - jnp.max(s, axis=0, keepdims=True))
            p = e * (1.0 / jnp.sum(e, axis=0, keepdims=True))
            gp = dot(v[:end], go, ((1,), (1,)))
            row_dot = jnp.sum(p * gp, axis=0, keepdims=True)
            gs = (p * (gp - row_dot) * FACTOR).astype(jnp.bfloat16)
            dv = dot(p.astype(jnp.bfloat16), go, ((1,), (0,)))
            dk = dot(gs, q, ((1,), (0,)))
            if block == half // ROWS - 1:
                v_acc[:end, :] = dv
                k_acc[:end, :] = dk
            else:
                v_acc[:end, :] += dv
                k_acc[:end, :] += dk
            dq = dot(k_turned[:, :end], gs, ((1,), (0,))).T
            dq_out[c, q_rows, lane] = dq.astype(jnp.bfloat16)
            at = pl.ds(part * chunk_heads + h, 1)
            sums_ref[at, :] += jnp.sum(dq, axis=0, keepdims=True)
        dk_out[c, :total, lane] = k_acc[:total, :].astype(jnp.bfloat16)
        dv_out[c, :total, lane] = v_acc[:total, :].astype(jnp.bfloat16)

    results = (dq_out, dk_out, dv_out)
    finals = (dq_hbm, k_low, v_low)

    def work(c, _):
        item, part = c // parts, lax.rem(c, parts)
        wait_bytes(q_in.at[c], in_recv.at[c, 0])
        wait_bytes(g_in.at[c], in_recv.at[c, 1])
        wait_bytes(k_in.at[c, :half], in_recv.at[c, 2])
        wait_bytes(v_in.at[c, :half], in_recv.at[c, 3])

        @pl.when(lower)
        def _():
            for h in range(chunk_heads):
                attend(c, part, h, 0)

        @pl.when(upper)
        def _():
            wait_bytes(k_in.at[c, :half], low_recv.at[c, 0])
            wait_bytes(v_in.at[c, :half], low_recv.at[c, 1])
            for h in range(chunk_heads):
                attend(c, part, h, half)

        def rows_of(a, to):
            start = to * rows if a == 0 else (base + to) * rows
            return results[a].at[c, pl.ds(pl.multiple_of(start, rows), rows)]

        def step(i, _):
            shift = (m - 1) - i // 2 - lax.rem(i, 2) * (m // 2)
            to = lax.rem(g + shift, m)

            @pl.when(upper)
            def _():
                for a, high in ((1, k_high), (2, v_high)):
                    remote(
                        results[a].at[c, pl.ds(pl.multiple_of(to * rows, rows), rows)],
                        high.at[item, :, column(g, part)],
                        high_send.at[c, a - 1], high_recv.at[c, a - 1], to,
                    )

            @pl.when(shift > 0)
            def _():
                for a in range(3):
                    remote(
                        rows_of(a, to), finals[a].at[item, :, column(g, part)],
                        out_send.at[c, a], out_recv.at[c, a], base + to,
                    )
            return 0

        lax.fori_loop(0, m, step, 0)
        for a in range(3):
            pltpu.make_async_copy(
                rows_of(a, g), finals[a].at[item, :, column(g, part)], out_recv.at[c, a]
            ).start()
        return 0

    lax.fori_loop(0, chunks, work, 0)

    def arrived(c, _):
        for a in range(3):
            wait_bytes(finals[a].at[0, :, pl.ds(0, m * cols)], out_recv.at[c, a])

        @pl.when(lower)
        def _():
            for a, high in ((0, k_high), (1, v_high)):
                wait_bytes(high.at[0, :, pl.ds(0, m * cols)], high_recv.at[c, a])
        return 0

    lax.fori_loop(0, chunks, arrived, 0)

    @pl.when(lower)
    def _():
        for low, high in ((k_low, k_high), (v_low, v_high)):
            def add(i, _):
                piece = pl.ds(pl.multiple_of(i * 16, 16), 16)
                for item in range(items):
                    low[item, piece, :] = (
                        low[item, piece, :].astype(jnp.float32)
                        + high[item, piece, :].astype(jnp.float32)
                    ).astype(jnp.bfloat16)
                return 0

            lax.fori_loop(0, rows // 16, add, 0)

    ends = [
        pltpu.make_async_copy(low, out, last_sem.at[i])
        for i, (low, out) in enumerate(((k_low, dk_hbm), (v_low, dv_hbm)))
    ]
    for copy in ends:
        copy.start()

    def sent(c, _):
        less = (m - 1) * rows
        for a in range(4):
            wait_bytes(q_in.at[c, pl.ds(0, less)], in_send.at[c, a])
        for a in range(3):
            wait_bytes(dq_out.at[c, pl.ds(0, less)], out_send.at[c, a])

        @pl.when(lower)
        def _():
            for a in range(2):
                wait_bytes(q_in.at[c], low_send.at[c, a])

        @pl.when(upper)
        def _():
            for a in range(2):
                wait_bytes(dq_out.at[c], high_send.at[c, a])
        return 0

    lax.fori_loop(0, chunks, sent, 0)
    for copy in ends:
        copy.wait()


def body(n, queries, key_states, value_states, grad_output, query_bias):
    items, rows, width = queries.shape
    m = n // 2
    heads = width // HDIM // m
    parts = 2
    chunk_heads = heads // parts
    cols = chunk_heads * HDIM
    half = m * rows
    chunks = items * parts
    bf16, f32 = jnp.bfloat16, jnp.float32
    own = heads * HDIM
    group = lax.rem(lax.axis_index("seq"), m)

    whole_bias = lax.all_gather(query_bias, ("seq", "dp"), axis=0, tiled=True)
    bias = lax.dynamic_slice(whole_bias, (group * own,), (own,))
    bias = bias.astype(f32).reshape(heads, HDIM)

    result = jax.ShapeDtypeStruct(queries.shape, bf16)
    dma = pltpu.SemaphoreType.DMA
    anywhere = pl.BlockSpec(memory_space=pl.ANY)
    local = pl.BlockSpec(memory_space=pltpu.VMEM)
    grad_queries, grad_keys, grad_values, sums = pl.pallas_call(
        functools.partial(kernel, n, chunk_heads, parts),
        out_shape=(result, result, result, jax.ShapeDtypeStruct((heads, HDIM), f32)),
        in_specs=[anywhere] * 4 + [local],
        out_specs=(anywhere, anywhere, anywhere, local),
        scratch_shapes=[
            pltpu.VMEM((chunks, half, cols), bf16),
            pltpu.VMEM((chunks, half, cols), bf16),
            pltpu.VMEM((chunks, 2 * half, cols), bf16),
            pltpu.VMEM((chunks, 2 * half, cols), bf16),
            pltpu.VMEM((chunks, half, cols), bf16),
            pltpu.VMEM((chunks, 2 * half, cols), bf16),
            pltpu.VMEM((chunks, 2 * half, cols), bf16),
            pltpu.VMEM(queries.shape, bf16),
            pltpu.VMEM(queries.shape, bf16),
            pltpu.VMEM(queries.shape, bf16),
            pltpu.VMEM(queries.shape, bf16),
            pltpu.VMEM((2 * half, HDIM), f32),
            pltpu.VMEM((2 * half, HDIM), f32),
            dma((chunks, 4)), dma((chunks, 4)), dma((chunks, 2)), dma((chunks, 2)),
            dma((chunks, 3)), dma((chunks, 3)), dma((chunks, 2)), dma((chunks, 2)),
            dma((2,)),
        ],
        compiler_params=pltpu.CompilerParams(
            collective_id=0, has_side_effects=True, vmem_limit_bytes=52 * 1024 * 1024
        ),
    )(queries, key_states, value_states, grad_output, bias)

    bias_total = lax.dynamic_update_slice(
        jnp.zeros((width,), f32), sums.reshape(own), (group * own,)
    )
    grad_bias = lax.psum_scatter(bias_total, ("seq", "dp"), scatter_dimension=0, tiled=True)
    return (grad_queries, grad_keys, grad_values, grad_bias)


def solution(mesh):
    in_specs = (
        P("dp", "seq", None),
        P("dp", "seq", None),
        P("dp", "seq", None),
        P("dp", "seq", None),
        P(("seq", "dp")),
    )
    out_specs = (P("dp", "seq", None), P("dp", "seq", None), P("dp", "seq", None), P(("seq", "dp")))
    return jax.shard_map(
        functools.partial(body, mesh.shape["seq"]),
        mesh=mesh, in_specs=in_specs, out_specs=out_specs, check_vma=False,
    )
```

```python
import functools
import math

import jax
import jax.numpy as jnp
from jax import lax
from jax.experimental import pallas as pl
from jax.experimental.pallas import tpu as pltpu
from jax.sharding import PartitionSpec as P

HDIM = 128
ROWS = 256
FACTOR = 1.0 / math.sqrt(HDIM)
MESH = pl.DeviceIdType.MESH


def dot(a, b, dims):
    return lax.dot_general(a, b, (dims, ((), ())), preferred_element_type=jnp.float32)


def wait_bytes(ref, sem):
    pltpu.make_async_copy(ref, ref, sem).wait()


def kernel(
    n, cores, chunk_heads, parts, exchange,
    q_hbm, k_hbm, v_hbm, g_hbm, bias_ref,
    dq_hbm, dk_hbm, dv_hbm, sums_ref,
    q_in, g_in, k_in, v_in,
    dq_out, dk_out, dv_out,
    k_low, v_low, k_high, v_high,
    k_acc, v_acc, bias_in, sums_acc, sums_in,
    in_recv, in_send, low_recv, low_send,
    out_recv, out_send, high_recv, high_send, last_sem,
    bias_recv, bias_send, sums_recv, sums_send,
):
    m = n // 2
    me = lax.axis_index("seq")
    upper = me >= m
    lower = me < m
    g = lax.rem(me, m)
    base = me - g
    items, rows, _ = q_hbm.shape
    half = m * rows
    cols = chunk_heads * HDIM
    own = parts * cols
    chunks = items * parts

    heads = parts * chunk_heads
    core = lax.axis_index("dp")
    flat = me * cores + core

    barrier = pltpu.get_barrier_semaphore()

    def greet(i, _):
        if exchange:
            other = lax.rem(flat + i, n * cores)
            target = {"seq": other // cores, "dp": lax.rem(other, cores)}
        else:
            target = {"seq": lax.rem(me + i, n)}
        pl.semaphore_signal(barrier, inc=1, device_id=target, device_id_type=MESH)
        return 0

    greeted = n * cores if exchange else n
    lax.fori_loop(1, greeted, greet, 0)
    pl.semaphore_wait(barrier, greeted - 1)

    owned = flat // heads
    workers = [(side * m + owned, dp) for side in range(2) for dp in range(cores)]
    owners = [
        ((g * heads + j) // cores, lax.rem(g * heads + j, cores)) for j in range(heads)
    ]

    def hand_out(targets, src_of, dst, recv, sends):
        for i, (seq, dp) in enumerate(targets):
            away = seq * cores + dp != flat

            @pl.when(away)
            def _():
                pltpu.make_async_remote_copy(
                    src_ref=src_of(i), dst_ref=dst, send_sem=sends.at[i], recv_sem=recv,
                    device_id={"seq": seq, "dp": dp}, device_id_type=MESH,
                ).start()

            @pl.when(jnp.logical_not(away))
            def _():
                pltpu.make_async_copy(src_of(i), dst, recv).start()

    def handed_out(targets, ref, sends):
        for i, (seq, dp) in enumerate(targets):
            @pl.when(seq * cores + dp != flat)
            def _():
                wait_bytes(ref.at[0], sends.at[i])

    if exchange:
        hand_out(
            workers, lambda i: bias_ref, bias_in.at[lax.rem(flat, heads)],
            bias_recv.at[0], bias_send,
        )

    def column(owner, part):
        return pl.ds(pl.multiple_of(owner * own + part * cols, 128), cols)

    def remote(src, dst, send, recv, peer):
        pltpu.make_async_remote_copy(
            src_ref=src, dst_ref=dst, send_sem=send, recv_sem=recv,
            device_id={"seq": peer}, device_id_type=MESH,
        ).start()

    sources = (q_hbm, g_hbm, k_hbm, v_hbm)
    landing = (q_in, g_in, k_in, v_in)

    def send_inputs(c, _):
        item, part = c // parts, lax.rem(c, parts)
        mine = pl.ds(pl.multiple_of(g * rows, rows), rows)
        at = pl.ds(pl.multiple_of(me * rows, rows), rows)

        def place(a):
            return landing[a].at[c, mine if a < 2 else at]

        def step(i, _):
            shift = (m - 1) - i // 2 - lax.rem(i, 2) * (m // 2)
            to = lax.rem(g + shift, m)

            @pl.when(lower)
            def _():
                for a in (2, 3):
                    remote(
                        sources[a].at[item, :, column(to, part)], landing[a].at[c, at],
                        low_send.at[c, a - 2], low_recv.at[c, a - 2], m + to,
                    )

            @pl.when(shift > 0)
            def _():
                for a in (2, 3, 0, 1):
                    remote(
                        sources[a].at[item, :, column(to, part)], place(a),
                        in_send.at[c, a], in_recv.at[c, a], base + to,
                    )
            return 0

        lax.fori_loop(0, m, step, 0)
        for a in range(4):
            pltpu.make_async_copy(
                sources[a].at[item, :, column(g, part)], place(a), in_recv.at[c, a]
            ).start()
        return 0

    lax.fori_loop(0, chunks, send_inputs, 0)
    sums_acc[...] = jnp.zeros_like(sums_acc)
    if exchange:
        wait_bytes(bias_in, bias_recv.at[0])

    def attend(c, part, h, offset):
        lane = pl.ds(h * HDIM, HDIM)
        total = offset + half
        k = k_in[c, :total, lane]
        v = v_in[c, :total, lane]
        k_turned = k.astype(jnp.float32).T.astype(jnp.bfloat16)
        head = part * chunk_heads + h
        bias = bias_in[head, :1, :] if exchange else bias_ref[head, :1, :]
        for block in reversed(range(half // ROWS)):
            q_rows = pl.ds(block * ROWS, ROWS)
            end = offset + (block + 1) * ROWS
            q = (q_in[c, q_rows, lane].astype(jnp.float32) + bias).astype(jnp.bfloat16)
            go = g_in[c, q_rows, lane]
            s = dot(k[:end], q, ((1,), (1,))) * FACTOR
            key_ids = lax.broadcasted_iota(jnp.int32, (ROWS, ROWS), 0)
            row_ids = lax.broadcasted_iota(jnp.int32, (ROWS, ROWS), 1)
            corner = jnp.where(key_ids <= row_ids, s[end - ROWS:], -1e30)
            s = corner if end == ROWS else jnp.concatenate([s[:end - ROWS], corner], axis=0)
            e = jnp.exp(s - jnp.max(s, axis=0, keepdims=True))
            p = e * (1.0 / jnp.sum(e, axis=0, keepdims=True))
            gp = dot(v[:end], go, ((1,), (1,)))
            row_dot = jnp.sum(p * gp, axis=0, keepdims=True)
            gs = (p * (gp - row_dot) * FACTOR).astype(jnp.bfloat16)
            dv = dot(p.astype(jnp.bfloat16), go, ((1,), (0,)))
            dk = dot(gs, q, ((1,), (0,)))
            if block == half // ROWS - 1:
                v_acc[:end, :] = dv
                k_acc[:end, :] = dk
            else:
                v_acc[:end, :] += dv
                k_acc[:end, :] += dk
            dq = dot(k_turned[:, :end], gs, ((1,), (0,))).T
            dq_out[c, q_rows, lane] = dq.astype(jnp.bfloat16)
            sums_acc[head] += jnp.sum(dq.reshape(ROWS // 8, 8, HDIM), axis=0)
        dk_out[c, :total, lane] = k_acc[:total, :].astype(jnp.bfloat16)
        dv_out[c, :total, lane] = v_acc[:total, :].astype(jnp.bfloat16)

    results = (dq_out, dk_out, dv_out)
    finals = (dq_hbm, k_low, v_low)

    def work(c, _):
        item, part = c // parts, lax.rem(c, parts)
        wait_bytes(q_in.at[c], in_recv.at[c, 0])
        wait_bytes(g_in.at[c], in_recv.at[c, 1])
        wait_bytes(k_in.at[c, :half], in_recv.at[c, 2])
        wait_bytes(v_in.at[c, :half], in_recv.at[c, 3])

        @pl.when(lower)
        def _():
            for h in range(chunk_heads):
                attend(c, part, h, 0)

        @pl.when(upper)
        def _():
            wait_bytes(k_in.at[c, :half], low_recv.at[c, 0])
            wait_bytes(v_in.at[c, :half], low_recv.at[c, 1])
            for h in range(chunk_heads):
                attend(c, part, h, half)

        def rows_of(a, to):
            start = to * rows if a == 0 else (base + to) * rows
            return results[a].at[c, pl.ds(pl.multiple_of(start, rows), rows)]

        def step(i, _):
            shift = (m - 1) - i // 2 - lax.rem(i, 2) * (m // 2)
            to = lax.rem(g + shift, m)

            @pl.when(upper)
            def _():
                for a, high in ((1, k_high), (2, v_high)):
                    remote(
                        results[a].at[c, pl.ds(pl.multiple_of(to * rows, rows), rows)],
                        high.at[item, :, column(g, part)],
                        high_send.at[c, a - 1], high_recv.at[c, a - 1], to,
                    )

            @pl.when(shift > 0)
            def _():
                for a in range(3):
                    remote(
                        rows_of(a, to), finals[a].at[item, :, column(g, part)],
                        out_send.at[c, a], out_recv.at[c, a], base + to,
                    )
            return 0

        lax.fori_loop(0, m, step, 0)
        for a in range(3):
            pltpu.make_async_copy(
                rows_of(a, g), finals[a].at[item, :, column(g, part)], out_recv.at[c, a]
            ).start()
        return 0

    lax.fori_loop(0, chunks, work, 0)

    if exchange:
        hand_out(
            owners, lambda j: sums_acc.at[j], sums_in.at[(me // m) * cores + core],
            sums_recv.at[0], sums_send,
        )

    def arrived(c, _):
        for a in range(3):
            wait_bytes(finals[a].at[0, :, pl.ds(0, m * cols)], out_recv.at[c, a])

        @pl.when(lower)
        def _():
            for a, high in ((0, k_high), (1, v_high)):
                wait_bytes(high.at[0, :, pl.ds(0, m * cols)], high_recv.at[c, a])
        return 0

    lax.fori_loop(0, chunks, arrived, 0)

    @pl.when(lower)
    def _():
        for low, high in ((k_low, k_high), (v_low, v_high)):
            def add(i, _):
                piece = pl.ds(pl.multiple_of(i * 16, 16), 16)
                for item in range(items):
                    low[item, piece, :] = (
                        low[item, piece, :].astype(jnp.float32)
                        + high[item, piece, :].astype(jnp.float32)
                    ).astype(jnp.bfloat16)
                return 0

            lax.fori_loop(0, rows // 16, add, 0)

    ends = [
        pltpu.make_async_copy(low, out, last_sem.at[i])
        for i, (low, out) in enumerate(((k_low, dk_hbm), (v_low, dv_hbm)))
    ]
    for copy in ends:
        copy.start()

    def sent(c, _):
        less = (m - 1) * rows
        for a in range(4):
            wait_bytes(q_in.at[c, pl.ds(0, less)], in_send.at[c, a])
        for a in range(3):
            wait_bytes(dq_out.at[c, pl.ds(0, less)], out_send.at[c, a])

        @pl.when(lower)
        def _():
            for a in range(2):
                wait_bytes(q_in.at[c], low_send.at[c, a])

        @pl.when(upper)
        def _():
            for a in range(2):
                wait_bytes(dq_out.at[c], high_send.at[c, a])
        return 0

    lax.fori_loop(0, chunks, sent, 0)
    if exchange:
        wait_bytes(sums_in, sums_recv.at[0])
        sums_ref[...] = jnp.sum(jnp.sum(sums_in[...], axis=0), axis=0, keepdims=True)
        handed_out(workers, bias_in, bias_send)
        handed_out(owners, sums_acc, sums_send)
    else:
        sums_ref[...] = jnp.sum(sums_acc[...], axis=1)
    for copy in ends:
        copy.wait()


def body(n, cores, queries, key_states, value_states, grad_output, query_bias):
    items, rows, width = queries.shape
    m = n // 2
    heads = width // HDIM // m
    parts = 2
    chunk_heads = heads // parts
    cols = chunk_heads * HDIM
    half = m * rows
    chunks = items * parts
    bf16, f32 = jnp.bfloat16, jnp.float32
    own = heads * HDIM
    group = lax.rem(lax.axis_index("seq"), m)

    exchange = width == HDIM * n * cores
    if exchange:
        bias = jnp.broadcast_to(query_bias.astype(f32)[None, :], (8, HDIM))
        sums_rows = 1
    else:
        whole_bias = lax.all_gather(query_bias, ("seq", "dp"), axis=0, tiled=True)
        bias = lax.dynamic_slice(whole_bias, (group * own,), (own,))
        bias = bias.astype(f32).reshape(heads, 1, HDIM)
        sums_rows = heads

    result = jax.ShapeDtypeStruct(queries.shape, bf16)
    dma = pltpu.SemaphoreType.DMA
    anywhere = pl.BlockSpec(memory_space=pl.ANY)
    local = pl.BlockSpec(memory_space=pltpu.VMEM)
    grad_queries, grad_keys, grad_values, sums = pl.pallas_call(
        functools.partial(kernel, n, cores, chunk_heads, parts, exchange),
        out_shape=(result, result, result, jax.ShapeDtypeStruct((sums_rows, HDIM), f32)),
        in_specs=[anywhere] * 4 + [local],
        out_specs=(anywhere, anywhere, anywhere, local),
        scratch_shapes=[
            pltpu.VMEM((chunks, half, cols), bf16),
            pltpu.VMEM((chunks, half, cols), bf16),
            pltpu.VMEM((chunks, 2 * half, cols), bf16),
            pltpu.VMEM((chunks, 2 * half, cols), bf16),
            pltpu.VMEM((chunks, half, cols), bf16),
            pltpu.VMEM((chunks, 2 * half, cols), bf16),
            pltpu.VMEM((chunks, 2 * half, cols), bf16),
            pltpu.VMEM(queries.shape, bf16),
            pltpu.VMEM(queries.shape, bf16),
            pltpu.VMEM(queries.shape, bf16),
            pltpu.VMEM(queries.shape, bf16),
            pltpu.VMEM((2 * half, HDIM), f32),
            pltpu.VMEM((2 * half, HDIM), f32),
            pltpu.VMEM((heads, 8, HDIM), f32),
            pltpu.VMEM((heads, 8, HDIM), f32),
            pltpu.VMEM((2 * cores, 8, HDIM), f32),
            dma((chunks, 4)), dma((chunks, 4)), dma((chunks, 2)), dma((chunks, 2)),
            dma((chunks, 3)), dma((chunks, 3)), dma((chunks, 2)), dma((chunks, 2)),
            dma((2,)), dma((1,)), dma((2 * cores,)), dma((1,)), dma((heads,)),
        ],
        compiler_params=pltpu.CompilerParams(
            collective_id=0, has_side_effects=True, vmem_limit_bytes=52 * 1024 * 1024
        ),
    )(queries, key_states, value_states, grad_output, bias)

    if exchange:
        return (grad_queries, grad_keys, grad_values, sums.reshape(HDIM))
    bias_total = lax.dynamic_update_slice(
        jnp.zeros((width,), f32), sums.reshape(own), (group * own,)
    )
    grad_bias = lax.psum_scatter(bias_total, ("seq", "dp"), scatter_dimension=0, tiled=True)
    return (grad_queries, grad_keys, grad_values, grad_bias)


def solution(mesh):
    in_specs = (
        P("dp", "seq", None),
        P("dp", "seq", None),
        P("dp", "seq", None),
        P("dp", "seq", None),
        P(("seq", "dp")),
    )
    out_specs = (P("dp", "seq", None), P("dp", "seq", None), P("dp", "seq", None), P(("seq", "dp")))
    return jax.shard_map(
        functools.partial(body, mesh.shape["seq"], mesh.shape["dp"]),
        mesh=mesh, in_specs=in_specs, out_specs=out_specs, check_vma=False,
    )
```

```python
import functools
import math

import jax
import jax.numpy as jnp
from jax import lax
from jax.experimental import pallas as pl
from jax.experimental.pallas import tpu as pltpu
from jax.sharding import PartitionSpec as P

HDIM = 128
ROWS = 256
FACTOR = 1.0 / math.sqrt(HDIM)
MESH = pl.DeviceIdType.MESH


def dot(a, b, dims):
    return lax.dot_general(a, b, (dims, ((), ())), preferred_element_type=jnp.float32)


def wait_bytes(ref, sem):
    pltpu.make_async_copy(ref, ref, sem).wait()


def kernel(
    n, cores, chunk_heads, parts, exchange,
    q_hbm, k_hbm, v_hbm, g_hbm, bias_ref,
    dq_hbm, dk_hbm, dv_hbm, sums_ref,
    q_in, g_in, k_in, v_in,
    dq_out, dk_out, dv_out,
    k_low, v_low, k_high, v_high,
    k_acc, v_acc, bias_in, sums_acc, sums_in,
    in_recv, in_send, low_recv, low_send,
    out_recv, out_send, high_recv, high_send, last_sem,
    bias_recv, bias_send, sums_recv, sums_send,
):
    m = n // 2
    me = lax.axis_index("seq")
    upper = me >= m
    lower = me < m
    g = lax.rem(me, m)
    base = me - g
    items, rows, _ = q_hbm.shape
    half = m * rows
    cols = chunk_heads * HDIM
    own = parts * cols
    chunks = items * parts

    heads = parts * chunk_heads
    core = lax.axis_index("dp")
    flat = me * cores + core

    barrier = pltpu.get_barrier_semaphore()

    def greet(i, _):
        if exchange:
            other = lax.rem(flat + i, n * cores)
            target = {"seq": other // cores, "dp": lax.rem(other, cores)}
        else:
            target = {"seq": lax.rem(me + i, n)}
        pl.semaphore_signal(barrier, inc=1, device_id=target, device_id_type=MESH)
        return 0

    greeted = n * cores if exchange else n
    lax.fori_loop(1, greeted, greet, 0)
    pl.semaphore_wait(barrier, greeted - 1)

    owned = flat // heads
    workers = [(side * m + owned, dp) for side in range(2) for dp in range(cores)]
    owners = [
        ((g * heads + j) // cores, lax.rem(g * heads + j, cores)) for j in range(heads)
    ]

    def hand_out(targets, src_of, dst, recv, sends):
        for i, (seq, dp) in enumerate(targets):
            away = seq * cores + dp != flat

            @pl.when(away)
            def _():
                pltpu.make_async_remote_copy(
                    src_ref=src_of(i), dst_ref=dst, send_sem=sends.at[i], recv_sem=recv,
                    device_id={"seq": seq, "dp": dp}, device_id_type=MESH,
                ).start()

            @pl.when(jnp.logical_not(away))
            def _():
                pltpu.make_async_copy(src_of(i), dst, recv).start()

    def handed_out(targets, ref, sends):
        for i, (seq, dp) in enumerate(targets):
            @pl.when(seq * cores + dp != flat)
            def _():
                wait_bytes(ref.at[0], sends.at[i])

    if exchange:
        hand_out(
            workers, lambda i: bias_ref, bias_in.at[lax.rem(flat, heads)],
            bias_recv.at[0], bias_send,
        )

    def column(owner, part):
        return pl.ds(pl.multiple_of(owner * own + part * cols, 128), cols)

    def remote(src, dst, send, recv, peer):
        pltpu.make_async_remote_copy(
            src_ref=src, dst_ref=dst, send_sem=send, recv_sem=recv,
            device_id={"seq": peer}, device_id_type=MESH,
        ).start()

    sources = (q_hbm, g_hbm, k_hbm, v_hbm)
    landing = (q_in, g_in, k_in, v_in)

    def send_inputs(c, _):
        item, part = c // parts, lax.rem(c, parts)
        mine = pl.ds(pl.multiple_of(g * rows, rows), rows)
        at = pl.ds(pl.multiple_of(me * rows, rows), rows)

        def place(a):
            return landing[a].at[c, mine if a < 2 else at]

        def step(i, _):
            shift = (m - 1) - i // 2 - lax.rem(i, 2) * (m // 2)
            to = lax.rem(g + shift, m)

            @pl.when(lower)
            def _():
                for a in (2, 3):
                    remote(
                        sources[a].at[item, :, column(to, part)], landing[a].at[c, at],
                        low_send.at[c, a - 2], low_recv.at[c, a - 2], m + to,
                    )

            @pl.when(shift > 0)
            def _():
                for a in (2, 3, 0, 1):
                    remote(
                        sources[a].at[item, :, column(to, part)], place(a),
                        in_send.at[c, a], in_recv.at[c, a], base + to,
                    )
            return 0

        lax.fori_loop(0, m, step, 0)
        for a in range(4):
            pltpu.make_async_copy(
                sources[a].at[item, :, column(g, part)], place(a), in_recv.at[c, a]
            ).start()
        return 0

    lax.fori_loop(0, chunks, send_inputs, 0)
    sums_acc[...] = jnp.zeros_like(sums_acc)
    if exchange:
        wait_bytes(bias_in, bias_recv.at[0])

    def attend(c, part, h, offset):
        lane = pl.ds(h * HDIM, HDIM)
        total = offset + half
        k = k_in[c, :total, lane]
        v = v_in[c, :total, lane]
        k_turned = k.astype(jnp.float32).T.astype(jnp.bfloat16)
        head = part * chunk_heads + h
        bias = bias_in[head, :1, :] if exchange else bias_ref[head, :1, :]
        for block in reversed(range(half // ROWS)):
            q_rows = pl.ds(block * ROWS, ROWS)
            end = offset + (block + 1) * ROWS
            q = (q_in[c, q_rows, lane].astype(jnp.float32) + bias).astype(jnp.bfloat16)
            go = g_in[c, q_rows, lane]
            s = dot(k[:end], q, ((1,), (1,))) * FACTOR
            key_ids = lax.broadcasted_iota(jnp.int32, (ROWS, ROWS), 0)
            row_ids = lax.broadcasted_iota(jnp.int32, (ROWS, ROWS), 1)
            corner = jnp.where(key_ids <= row_ids, s[end - ROWS:], -1e30)
            s = corner if end == ROWS else jnp.concatenate([s[:end - ROWS], corner], axis=0)
            e = jnp.exp(s - jnp.max(s, axis=0, keepdims=True))
            p = e * (1.0 / jnp.sum(e, axis=0, keepdims=True))
            gp = dot(v[:end], go, ((1,), (1,)))
            row_dot = jnp.sum(p * gp, axis=0, keepdims=True)
            gs = (p * (gp - row_dot) * FACTOR).astype(jnp.bfloat16)
            dv = dot(p.astype(jnp.bfloat16), go, ((1,), (0,)))
            dk = dot(gs, q, ((1,), (0,)))
            if block == half // ROWS - 1:
                v_acc[:end, :] = dv
                k_acc[:end, :] = dk
            else:
                v_acc[:end, :] += dv
                k_acc[:end, :] += dk
            dq = dot(k_turned[:, :end], gs, ((1,), (0,))).T
            dq_out[c, q_rows, lane] = dq.astype(jnp.bfloat16)
            sums_acc[head] += jnp.sum(dq.reshape(ROWS // 8, 8, HDIM), axis=0)
        dk_out[c, :total, lane] = k_acc[:total, :].astype(jnp.bfloat16)
        dv_out[c, :total, lane] = v_acc[:total, :].astype(jnp.bfloat16)

    results = (dq_out, dk_out, dv_out)
    finals = (dq_hbm, k_low, v_low)

    def work(c, _):
        item, part = c // parts, lax.rem(c, parts)
        wait_bytes(q_in.at[c], in_recv.at[c, 0])
        wait_bytes(g_in.at[c], in_recv.at[c, 1])
        wait_bytes(k_in.at[c, :half], in_recv.at[c, 2])
        wait_bytes(v_in.at[c, :half], in_recv.at[c, 3])

        @pl.when(lower)
        def _():
            for h in range(chunk_heads):
                attend(c, part, h, 0)

        @pl.when(upper)
        def _():
            wait_bytes(k_in.at[c, :half], low_recv.at[c, 0])
            wait_bytes(v_in.at[c, :half], low_recv.at[c, 1])
            for h in range(chunk_heads):
                attend(c, part, h, half)

        def rows_of(a, to):
            start = to * rows if a == 0 else (base + to) * rows
            return results[a].at[c, pl.ds(pl.multiple_of(start, rows), rows)]

        def step(i, _):
            shift = (m - 1) - i // 2 - lax.rem(i, 2) * (m // 2)
            to = lax.rem(g + shift, m)

            @pl.when(upper)
            def _():
                for a, high in ((1, k_high), (2, v_high)):
                    remote(
                        results[a].at[c, pl.ds(pl.multiple_of(to * rows, rows), rows)],
                        high.at[item, :, column(g, part)],
                        high_send.at[c, a - 1], high_recv.at[c, a - 1], to,
                    )

            @pl.when(shift > 0)
            def _():
                for a in range(3):
                    remote(
                        rows_of(a, to), finals[a].at[item, :, column(g, part)],
                        out_send.at[c, a], out_recv.at[c, a], base + to,
                    )
            return 0

        lax.fori_loop(0, m, step, 0)
        for a in range(3):
            pltpu.make_async_copy(
                rows_of(a, g), finals[a].at[item, :, column(g, part)], out_recv.at[c, a]
            ).start()
        return 0

    lax.fori_loop(0, chunks, work, 0)

    if exchange:
        hand_out(
            owners, lambda j: sums_acc.at[j], sums_in.at[(me // m) * cores + core],
            sums_recv.at[0], sums_send,
        )

    def arrived(c, _):
        for a in range(3):
            wait_bytes(finals[a].at[0, :, pl.ds(0, m * cols)], out_recv.at[c, a])

        @pl.when(lower)
        def _():
            for a, high in ((0, k_high), (1, v_high)):
                wait_bytes(high.at[0, :, pl.ds(0, m * cols)], high_recv.at[c, a])
        return 0

    lax.fori_loop(0, chunks, arrived, 0)

    @pl.when(lower)
    def _():
        for low, high in ((k_low, k_high), (v_low, v_high)):
            def add(i, _):
                piece = pl.ds(pl.multiple_of(i * 16, 16), 16)
                for item in range(items):
                    low[item, piece, :] = (
                        low[item, piece, :].astype(jnp.float32)
                        + high[item, piece, :].astype(jnp.float32)
                    ).astype(jnp.bfloat16)
                return 0

            lax.fori_loop(0, rows // 16, add, 0)

    ends = [
        pltpu.make_async_copy(low, out, last_sem.at[i])
        for i, (low, out) in enumerate(((k_low, dk_hbm), (v_low, dv_hbm)))
    ]
    for copy in ends:
        copy.start()

    def sent(c, _):
        less = (m - 1) * rows
        for a in range(4):
            wait_bytes(q_in.at[c, pl.ds(0, less)], in_send.at[c, a])
        for a in range(3):
            wait_bytes(dq_out.at[c, pl.ds(0, less)], out_send.at[c, a])

        @pl.when(lower)
        def _():
            for a in range(2):
                wait_bytes(q_in.at[c], low_send.at[c, a])

        @pl.when(upper)
        def _():
            for a in range(2):
                wait_bytes(dq_out.at[c], high_send.at[c, a])
        return 0

    lax.fori_loop(0, chunks, sent, 0)
    if exchange:
        wait_bytes(sums_in, sums_recv.at[0])
        sums_ref[...] = jnp.sum(jnp.sum(sums_in[...], axis=0), axis=0, keepdims=True)
        handed_out(workers, bias_in, bias_send)
        handed_out(owners, sums_acc, sums_send)
    else:
        sums_ref[...] = jnp.sum(sums_acc[...], axis=1)
    for copy in ends:
        copy.wait()


def body(n, cores, queries, key_states, value_states, grad_output, query_bias):
    items, rows, width = queries.shape
    m = n // 2
    heads = width // HDIM // m
    parts = min(4, heads)
    chunk_heads = heads // parts
    cols = chunk_heads * HDIM
    half = m * rows
    chunks = items * parts
    bf16, f32 = jnp.bfloat16, jnp.float32
    own = heads * HDIM
    group = lax.rem(lax.axis_index("seq"), m)

    exchange = width == HDIM * n * cores
    if exchange:
        bias = jnp.broadcast_to(query_bias.astype(f32)[None, :], (8, HDIM))
        sums_rows = 1
    else:
        whole_bias = lax.all_gather(query_bias, ("seq", "dp"), axis=0, tiled=True)
        bias = lax.dynamic_slice(whole_bias, (group * own,), (own,))
        bias = bias.astype(f32).reshape(heads, 1, HDIM)
        sums_rows = heads

    result = jax.ShapeDtypeStruct(queries.shape, bf16)
    dma = pltpu.SemaphoreType.DMA
    anywhere = pl.BlockSpec(memory_space=pl.ANY)
    local = pl.BlockSpec(memory_space=pltpu.VMEM)
    grad_queries, grad_keys, grad_values, sums = pl.pallas_call(
        functools.partial(kernel, n, cores, chunk_heads, parts, exchange),
        out_shape=(result, result, result, jax.ShapeDtypeStruct((sums_rows, HDIM), f32)),
        in_specs=[anywhere] * 4 + [local],
        out_specs=(anywhere, anywhere, anywhere, local),
        scratch_shapes=[
            pltpu.VMEM((chunks, half, cols), bf16),
            pltpu.VMEM((chunks, half, cols), bf16),
            pltpu.VMEM((chunks, 2 * half, cols), bf16),
            pltpu.VMEM((chunks, 2 * half, cols), bf16),
            pltpu.VMEM((chunks, half, cols), bf16),
            pltpu.VMEM((chunks, 2 * half, cols), bf16),
            pltpu.VMEM((chunks, 2 * half, cols), bf16),
            pltpu.VMEM(queries.shape, bf16),
            pltpu.VMEM(queries.shape, bf16),
            pltpu.VMEM(queries.shape, bf16),
            pltpu.VMEM(queries.shape, bf16),
            pltpu.VMEM((2 * half, HDIM), f32),
            pltpu.VMEM((2 * half, HDIM), f32),
            pltpu.VMEM((heads, 8, HDIM), f32),
            pltpu.VMEM((heads, 8, HDIM), f32),
            pltpu.VMEM((2 * cores, 8, HDIM), f32),
            dma((chunks, 4)), dma((chunks, 4)), dma((chunks, 2)), dma((chunks, 2)),
            dma((chunks, 3)), dma((chunks, 3)), dma((chunks, 2)), dma((chunks, 2)),
            dma((2,)), dma((1,)), dma((2 * cores,)), dma((1,)), dma((heads,)),
        ],
        compiler_params=pltpu.CompilerParams(
            collective_id=0, has_side_effects=True, vmem_limit_bytes=52 * 1024 * 1024
        ),
    )(queries, key_states, value_states, grad_output, bias)

    if exchange:
        return (grad_queries, grad_keys, grad_values, sums.reshape(HDIM))
    bias_total = lax.dynamic_update_slice(
        jnp.zeros((width,), f32), sums.reshape(own), (group * own,)
    )
    grad_bias = lax.psum_scatter(bias_total, ("seq", "dp"), scatter_dimension=0, tiled=True)
    return (grad_queries, grad_keys, grad_values, grad_bias)


def solution(mesh):
    in_specs = (
        P("dp", "seq", None),
        P("dp", "seq", None),
        P("dp", "seq", None),
        P("dp", "seq", None),
        P(("seq", "dp")),
    )
    out_specs = (P("dp", "seq", None), P("dp", "seq", None), P("dp", "seq", None), P(("seq", "dp")))
    return jax.shard_map(
        functools.partial(body, mesh.shape["seq"], mesh.shape["dp"]),
        mesh=mesh, in_specs=in_specs, out_specs=out_specs, check_vma=False,
    )
```

```python
import functools
import math

import jax
import jax.numpy as jnp
from jax import lax
from jax.experimental import pallas as pl
from jax.experimental.pallas import tpu as pltpu
from jax.sharding import PartitionSpec as P

HDIM = 128
ROWS = 256
FACTOR = 1.0 / math.sqrt(HDIM)
MESH = pl.DeviceIdType.MESH


def dot(a, b, dims):
    return lax.dot_general(a, b, (dims, ((), ())), preferred_element_type=jnp.float32)


def wait_bytes(ref, sem):
    pltpu.make_async_copy(ref, ref, sem).wait()


def kernel(
    n, cores, chunk_heads, parts, exchange,
    q_hbm, k_hbm, v_hbm, g_hbm, bias_ref,
    dq_hbm, dk_hbm, dv_hbm, sums_ref,
    q_in, g_in, k_in, v_in,
    dq_out, dk_out, dv_out,
    k_low, v_low, k_high, v_high,
    k_acc, v_acc, bias_in, sums_acc, sums_in,
    in_recv, in_send, low_recv, low_send,
    out_recv, out_send, high_recv, high_send, last_sem,
    bias_recv, bias_send, sums_recv, sums_send,
):
    m = n // 2
    me = lax.axis_index("seq")
    upper = me >= m
    lower = me < m
    g = lax.rem(me, m)
    base = me - g
    items, rows, _ = q_hbm.shape
    half = m * rows
    cols = chunk_heads * HDIM
    own = parts * cols
    chunks = items * parts

    heads = parts * chunk_heads
    core = lax.axis_index("dp")
    flat = me * cores + core

    barrier = pltpu.get_barrier_semaphore()

    def greet(i, _):
        if exchange:
            other = lax.rem(flat + i, n * cores)
            target = {"seq": other // cores, "dp": lax.rem(other, cores)}
        else:
            target = {"seq": lax.rem(me + i, n)}
        pl.semaphore_signal(barrier, inc=1, device_id=target, device_id_type=MESH)
        return 0

    greeted = n * cores if exchange else n
    lax.fori_loop(1, greeted, greet, 0)
    pl.semaphore_wait(barrier, greeted - 1)

    owned = flat // heads
    workers = [(side * m + owned, dp) for side in range(2) for dp in range(cores)]
    owners = [
        ((g * heads + j) // cores, lax.rem(g * heads + j, cores)) for j in range(heads)
    ]

    def hand_out(targets, src_of, dst, recv, sends):
        for i, (seq, dp) in enumerate(targets):
            away = seq * cores + dp != flat

            @pl.when(away)
            def _():
                pltpu.make_async_remote_copy(
                    src_ref=src_of(i), dst_ref=dst, send_sem=sends.at[i], recv_sem=recv,
                    device_id={"seq": seq, "dp": dp}, device_id_type=MESH,
                ).start()

            @pl.when(jnp.logical_not(away))
            def _():
                pltpu.make_async_copy(src_of(i), dst, recv).start()

    def handed_out(targets, ref, sends):
        for i, (seq, dp) in enumerate(targets):
            @pl.when(seq * cores + dp != flat)
            def _():
                wait_bytes(ref.at[0], sends.at[i])

    if exchange:
        hand_out(
            workers, lambda i: bias_ref, bias_in.at[lax.rem(flat, heads)],
            bias_recv.at[0], bias_send,
        )

    def column(owner, part):
        return pl.ds(pl.multiple_of(owner * own + part * cols, 128), cols)

    def remote(src, dst, send, recv, peer):
        pltpu.make_async_remote_copy(
            src_ref=src, dst_ref=dst, send_sem=send, recv_sem=recv,
            device_id={"seq": peer}, device_id_type=MESH,
        ).start()

    sources = (q_hbm, g_hbm, k_hbm, v_hbm)
    landing = (q_in, g_in, k_in, v_in)

    def send_inputs(c, _):
        item, part = c // parts, lax.rem(c, parts)
        mine = pl.ds(pl.multiple_of(g * rows, rows), rows)
        at = pl.ds(pl.multiple_of(me * rows, rows), rows)

        def place(a):
            return landing[a].at[c, mine if a < 2 else at]

        def step(i, _):
            shift = (m - 1) - i // 2 - lax.rem(i, 2) * (m // 2)
            to = lax.rem(g + shift, m)

            @pl.when(lower)
            def _():
                for a in (2, 3):
                    remote(
                        sources[a].at[item, :, column(to, part)], landing[a].at[c, at],
                        low_send.at[c, a - 2], low_recv.at[c, a - 2], m + to,
                    )

            @pl.when(shift > 0)
            def _():
                for a in (2, 3, 0, 1):
                    remote(
                        sources[a].at[item, :, column(to, part)], place(a),
                        in_send.at[c, a], in_recv.at[c, a], base + to,
                    )
            return 0

        lax.fori_loop(0, m, step, 0)
        for a in range(4):
            pltpu.make_async_copy(
                sources[a].at[item, :, column(g, part)], place(a), in_recv.at[c, a]
            ).start()
        return 0

    lax.fori_loop(0, chunks, send_inputs, 0)
    sums_acc[...] = jnp.zeros_like(sums_acc)
    if exchange:
        wait_bytes(bias_in, bias_recv.at[0])

    def attend(c, part, h, offset):
        lane = pl.ds(h * HDIM, HDIM)
        total = offset + half
        k = k_in[c, :total, lane]
        v = v_in[c, :total, lane]
        k_turned = k.astype(jnp.float32).T.astype(jnp.bfloat16)
        head = part * chunk_heads + h
        bias = bias_in[head, :1, :] if exchange else bias_ref[head, :1, :]
        for block in reversed(range(half // ROWS)):
            q_rows = pl.ds(block * ROWS, ROWS)
            end = offset + (block + 1) * ROWS
            q = (q_in[c, q_rows, lane].astype(jnp.float32) + bias).astype(jnp.bfloat16)
            go = g_in[c, q_rows, lane]
            s = dot(k[:end], q, ((1,), (1,))) * FACTOR
            key_ids = lax.broadcasted_iota(jnp.int32, (ROWS, ROWS), 0)
            row_ids = lax.broadcasted_iota(jnp.int32, (ROWS, ROWS), 1)
            corner = jnp.where(key_ids <= row_ids, s[end - ROWS:], -1e30)
            s = corner if end == ROWS else jnp.concatenate([s[:end - ROWS], corner], axis=0)
            e = jnp.exp(s - jnp.max(s, axis=0, keepdims=True))
            p = e * (1.0 / jnp.sum(e, axis=0, keepdims=True))
            gp = dot(v[:end], go, ((1,), (1,)))
            row_dot = jnp.sum(p * gp, axis=0, keepdims=True)
            gs = (p * (gp - row_dot) * FACTOR).astype(jnp.bfloat16)
            dv = dot(p.astype(jnp.bfloat16), go, ((1,), (0,)))
            dk = dot(gs, q, ((1,), (0,)))
            if block == half // ROWS - 1:
                v_acc[:end, :] = dv
                k_acc[:end, :] = dk
            else:
                v_acc[:end, :] += dv
                k_acc[:end, :] += dk
            dq = dot(k_turned[:, :end], gs, ((1,), (0,))).T
            dq_out[c, q_rows, lane] = dq.astype(jnp.bfloat16)
            sums_acc[head] += jnp.sum(dq.reshape(ROWS // 8, 8, HDIM), axis=0)
        dk_out[c, :total, lane] = k_acc[:total, :].astype(jnp.bfloat16)
        dv_out[c, :total, lane] = v_acc[:total, :].astype(jnp.bfloat16)

    results = (dq_out, dk_out, dv_out)
    finals = (dq_hbm, k_low, v_low)

    def rows_of(a, c, to):
        start = to * rows if a == 0 else (base + to) * rows
        return results[a].at[c, pl.ds(pl.multiple_of(start, rows), rows)]

    def send_results(c, chosen, first):
        item, part = c // parts, lax.rem(c, parts)

        def step(i, _):
            shift = (m - 1) - i // 2 - lax.rem(i, 2) * (m // 2)
            to = lax.rem(g + shift, m)
            climbs = jnp.logical_and(to >= m // 2, g < m // 2)

            if first:
                @pl.when(upper)
                def _():
                    for a, high in ((1, k_high), (2, v_high)):
                        remote(
                            results[a].at[c, pl.ds(pl.multiple_of(to * rows, rows), rows)],
                            high.at[item, :, column(g, part)],
                            high_send.at[c, a - 1], high_recv.at[c, a - 1], to,
                        )

            @pl.when(jnp.logical_and(shift > 0, chosen(climbs)))
            def _():
                for a in range(3):
                    remote(
                        rows_of(a, c, to), finals[a].at[item, :, column(g, part)],
                        out_send.at[c, a], out_recv.at[c, a], base + to,
                    )
            return 0

        lax.fori_loop(0, m, step, 0)

    def work(c, _):
        item, part = c // parts, lax.rem(c, parts)
        wait_bytes(q_in.at[c], in_recv.at[c, 0])
        wait_bytes(g_in.at[c], in_recv.at[c, 1])
        wait_bytes(k_in.at[c, :half], in_recv.at[c, 2])
        wait_bytes(v_in.at[c, :half], in_recv.at[c, 3])

        @pl.when(lower)
        def _():
            for h in range(chunk_heads):
                attend(c, part, h, 0)

        @pl.when(upper)
        def _():
            wait_bytes(k_in.at[c, :half], low_recv.at[c, 0])
            wait_bytes(v_in.at[c, :half], low_recv.at[c, 1])
            for h in range(chunk_heads):
                attend(c, part, h, half)

        last = chunks - 1
        send_results(c, lambda climbs: jnp.logical_or(jnp.logical_not(climbs), c == last), True)

        @pl.when(c == last - 1)
        def _():
            def release(held, _):
                send_results(held, lambda climbs: climbs, False)
                return 0

            lax.fori_loop(0, last, release, 0)

        for a in range(3):
            pltpu.make_async_copy(
                rows_of(a, c, g), finals[a].at[item, :, column(g, part)], out_recv.at[c, a]
            ).start()
        return 0

    lax.fori_loop(0, chunks, work, 0)

    if exchange:
        hand_out(
            owners, lambda j: sums_acc.at[j], sums_in.at[(me // m) * cores + core],
            sums_recv.at[0], sums_send,
        )

    def arrived(c, _):
        item, part = c // parts, lax.rem(c, parts)
        for a in range(3):
            wait_bytes(finals[a].at[0, :, pl.ds(0, m * cols)], out_recv.at[c, a])

        @pl.when(lower)
        def _():
            for a, high in ((0, k_high), (1, v_high)):
                wait_bytes(high.at[0, :, pl.ds(0, m * cols)], high_recv.at[c, a])

            def add(owner, _):
                lanes = column(owner, part)
                for low, high in ((k_low, k_high), (v_low, v_high)):
                    low[item, :, lanes] = (
                        low[item, :, lanes].astype(jnp.float32)
                        + high[item, :, lanes].astype(jnp.float32)
                    ).astype(jnp.bfloat16)
                return 0

            lax.fori_loop(0, m, add, 0)
        return 0

    lax.fori_loop(0, chunks, arrived, 0)

    ends = [
        pltpu.make_async_copy(low, out, last_sem.at[i])
        for i, (low, out) in enumerate(((k_low, dk_hbm), (v_low, dv_hbm)))
    ]
    for copy in ends:
        copy.start()

    def sent(c, _):
        less = (m - 1) * rows
        for a in range(4):
            wait_bytes(q_in.at[c, pl.ds(0, less)], in_send.at[c, a])
        for a in range(3):
            wait_bytes(dq_out.at[c, pl.ds(0, less)], out_send.at[c, a])

        @pl.when(lower)
        def _():
            for a in range(2):
                wait_bytes(q_in.at[c], low_send.at[c, a])

        @pl.when(upper)
        def _():
            for a in range(2):
                wait_bytes(dq_out.at[c], high_send.at[c, a])
        return 0

    lax.fori_loop(0, chunks, sent, 0)
    if exchange:
        wait_bytes(sums_in, sums_recv.at[0])
        sums_ref[...] = jnp.sum(jnp.sum(sums_in[...], axis=0), axis=0, keepdims=True)
        handed_out(workers, bias_in, bias_send)
        handed_out(owners, sums_acc, sums_send)
    else:
        sums_ref[...] = jnp.sum(sums_acc[...], axis=1)
    for copy in ends:
        copy.wait()


def body(n, cores, queries, key_states, value_states, grad_output, query_bias):
    items, rows, width = queries.shape
    m = n // 2
    heads = width // HDIM // m
    parts = min(4, heads)
    chunk_heads = heads // parts
    cols = chunk_heads * HDIM
    half = m * rows
    chunks = items * parts
    bf16, f32 = jnp.bfloat16, jnp.float32
    own = heads * HDIM
    group = lax.rem(lax.axis_index("seq"), m)

    exchange = width == HDIM * n * cores
    if exchange:
        bias = jnp.broadcast_to(query_bias.astype(f32)[None, :], (8, HDIM))
        sums_rows = 1
    else:
        whole_bias = lax.all_gather(query_bias, ("seq", "dp"), axis=0, tiled=True)
        bias = lax.dynamic_slice(whole_bias, (group * own,), (own,))
        bias = bias.astype(f32).reshape(heads, 1, HDIM)
        sums_rows = heads

    result = jax.ShapeDtypeStruct(queries.shape, bf16)
    dma = pltpu.SemaphoreType.DMA
    anywhere = pl.BlockSpec(memory_space=pl.ANY)
    local = pl.BlockSpec(memory_space=pltpu.VMEM)
    grad_queries, grad_keys, grad_values, sums = pl.pallas_call(
        functools.partial(kernel, n, cores, chunk_heads, parts, exchange),
        out_shape=(result, result, result, jax.ShapeDtypeStruct((sums_rows, HDIM), f32)),
        in_specs=[anywhere] * 4 + [local],
        out_specs=(anywhere, anywhere, anywhere, local),
        scratch_shapes=[
            pltpu.VMEM((chunks, half, cols), bf16),
            pltpu.VMEM((chunks, half, cols), bf16),
            pltpu.VMEM((chunks, 2 * half, cols), bf16),
            pltpu.VMEM((chunks, 2 * half, cols), bf16),
            pltpu.VMEM((chunks, half, cols), bf16),
            pltpu.VMEM((chunks, 2 * half, cols), bf16),
            pltpu.VMEM((chunks, 2 * half, cols), bf16),
            pltpu.VMEM(queries.shape, bf16),
            pltpu.VMEM(queries.shape, bf16),
            pltpu.VMEM(queries.shape, bf16),
            pltpu.VMEM(queries.shape, bf16),
            pltpu.VMEM((2 * half, HDIM), f32),
            pltpu.VMEM((2 * half, HDIM), f32),
            pltpu.VMEM((heads, 8, HDIM), f32),
            pltpu.VMEM((heads, 8, HDIM), f32),
            pltpu.VMEM((2 * cores, 8, HDIM), f32),
            dma((chunks, 4)), dma((chunks, 4)), dma((chunks, 2)), dma((chunks, 2)),
            dma((chunks, 3)), dma((chunks, 3)), dma((chunks, 2)), dma((chunks, 2)),
            dma((2,)), dma((1,)), dma((2 * cores,)), dma((1,)), dma((heads,)),
        ],
        compiler_params=pltpu.CompilerParams(
            collective_id=0, has_side_effects=True, vmem_limit_bytes=52 * 1024 * 1024
        ),
    )(queries, key_states, value_states, grad_output, bias)

    if exchange:
        return (grad_queries, grad_keys, grad_values, sums.reshape(HDIM))
    bias_total = lax.dynamic_update_slice(
        jnp.zeros((width,), f32), sums.reshape(own), (group * own,)
    )
    grad_bias = lax.psum_scatter(bias_total, ("seq", "dp"), scatter_dimension=0, tiled=True)
    return (grad_queries, grad_keys, grad_values, grad_bias)


def solution(mesh):
    in_specs = (
        P("dp", "seq", None),
        P("dp", "seq", None),
        P("dp", "seq", None),
        P("dp", "seq", None),
        P(("seq", "dp")),
    )
    out_specs = (P("dp", "seq", None), P("dp", "seq", None), P("dp", "seq", None), P(("seq", "dp")))
    return jax.shard_map(
        functools.partial(body, mesh.shape["seq"], mesh.shape["dp"]),
        mesh=mesh, in_specs=in_specs, out_specs=out_specs, check_vma=False,
    )
```

```python
import functools
import math

import jax
import jax.numpy as jnp
from jax import lax
from jax.experimental import pallas as pl
from jax.experimental.pallas import tpu as pltpu
from jax.sharding import PartitionSpec as P

HDIM = 128
ROWS = 256
FACTOR = 1.0 / math.sqrt(HDIM)
AHEAD = 3
MESH = pl.DeviceIdType.MESH


def dot(a, b, dims):
    return lax.dot_general(a, b, (dims, ((), ())), preferred_element_type=jnp.float32)


def wait_bytes(ref, sem):
    pltpu.make_async_copy(ref, ref, sem).wait()


def kernel(
    n, cores, chunk_heads, parts, exchange,
    q_hbm, k_hbm, v_hbm, g_hbm, bias_ref,
    dq_hbm, dk_hbm, dv_hbm, sums_ref,
    q_in, g_in, k_in, v_in,
    dq_out, dk_out, dv_out,
    k_low, v_low, k_high, v_high,
    k_acc, v_acc, bias_in, sums_acc, sums_in,
    in_recv, in_send, low_recv, low_send,
    out_recv, out_send, high_recv, high_send, last_sem,
    bias_recv, bias_send, sums_recv, sums_send,
):
    m = n // 2
    me = lax.axis_index("seq")
    upper = me >= m
    lower = me < m
    g = lax.rem(me, m)
    base = me - g
    items, rows, _ = q_hbm.shape
    half = m * rows
    cols = chunk_heads * HDIM
    own = parts * cols
    chunks = items * parts

    heads = parts * chunk_heads
    core = lax.axis_index("dp")
    flat = me * cores + core

    barrier = pltpu.get_barrier_semaphore()

    def greet(i, _):
        if exchange:
            other = lax.rem(flat + i, n * cores)
            target = {"seq": other // cores, "dp": lax.rem(other, cores)}
        else:
            target = {"seq": lax.rem(me + i, n)}
        pl.semaphore_signal(barrier, inc=1, device_id=target, device_id_type=MESH)
        return 0

    greeted = n * cores if exchange else n
    lax.fori_loop(1, greeted, greet, 0)
    pl.semaphore_wait(barrier, greeted - 1)

    owned = flat // heads
    workers = [(side * m + owned, dp) for side in range(2) for dp in range(cores)]
    owners = [
        ((g * heads + j) // cores, lax.rem(g * heads + j, cores)) for j in range(heads)
    ]

    def hand_out(targets, src_of, dst, recv, sends):
        for i, (seq, dp) in enumerate(targets):
            away = seq * cores + dp != flat

            @pl.when(away)
            def _():
                pltpu.make_async_remote_copy(
                    src_ref=src_of(i), dst_ref=dst, send_sem=sends.at[i], recv_sem=recv,
                    device_id={"seq": seq, "dp": dp}, device_id_type=MESH,
                ).start()

            @pl.when(jnp.logical_not(away))
            def _():
                pltpu.make_async_copy(src_of(i), dst, recv).start()

    def handed_out(targets, ref, sends):
        for i, (seq, dp) in enumerate(targets):
            @pl.when(seq * cores + dp != flat)
            def _():
                wait_bytes(ref.at[0], sends.at[i])

    if exchange:
        hand_out(
            workers, lambda i: bias_ref, bias_in.at[lax.rem(flat, heads)],
            bias_recv.at[0], bias_send,
        )

    def column(owner, part):
        return pl.ds(pl.multiple_of(owner * own + part * cols, 128), cols)

    def remote(src, dst, send, recv, peer):
        pltpu.make_async_remote_copy(
            src_ref=src, dst_ref=dst, send_sem=send, recv_sem=recv,
            device_id={"seq": peer}, device_id_type=MESH,
        ).start()

    sources = (q_hbm, g_hbm, k_hbm, v_hbm)
    landing = (q_in, g_in, k_in, v_in)

    def send_inputs(c, _):
        item, part = c // parts, lax.rem(c, parts)
        mine = pl.ds(pl.multiple_of(g * rows, rows), rows)
        at = pl.ds(pl.multiple_of(me * rows, rows), rows)

        def place(a):
            return landing[a].at[c, mine if a < 2 else at]

        def step(i, _):
            shift = (m - 1) - i // 2 - lax.rem(i, 2) * (m // 2)
            to = lax.rem(g + shift, m)

            @pl.when(lower)
            def _():
                for a in (2, 3):
                    remote(
                        sources[a].at[item, :, column(to, part)], landing[a].at[c, at],
                        low_send.at[c, a - 2], low_recv.at[c, a - 2], m + to,
                    )

            @pl.when(shift > 0)
            def _():
                for a in (2, 3, 0, 1):
                    remote(
                        sources[a].at[item, :, column(to, part)], place(a),
                        in_send.at[c, a], in_recv.at[c, a], base + to,
                    )
            return 0

        lax.fori_loop(0, m, step, 0)
        for a in range(4):
            pltpu.make_async_copy(
                sources[a].at[item, :, column(g, part)], place(a), in_recv.at[c, a]
            ).start()
        return 0

    lax.fori_loop(0, min(AHEAD, chunks), send_inputs, 0)
    sums_acc[...] = jnp.zeros_like(sums_acc)
    if exchange:
        wait_bytes(bias_in, bias_recv.at[0])

    def attend(c, part, h, offset):
        lane = pl.ds(h * HDIM, HDIM)
        total = offset + half
        k = k_in[c, :total, lane]
        v = v_in[c, :total, lane]
        k_turned = k.astype(jnp.float32).T.astype(jnp.bfloat16)
        head = part * chunk_heads + h
        bias = bias_in[head, :1, :] if exchange else bias_ref[head, :1, :]
        for block in reversed(range(half // ROWS)):
            q_rows = pl.ds(block * ROWS, ROWS)
            end = offset + (block + 1) * ROWS
            q = (q_in[c, q_rows, lane].astype(jnp.float32) + bias).astype(jnp.bfloat16)
            go = g_in[c, q_rows, lane]
            s = dot(k[:end], q, ((1,), (1,)))
            key_ids = lax.broadcasted_iota(jnp.int32, (ROWS, ROWS), 0)
            row_ids = lax.broadcasted_iota(jnp.int32, (ROWS, ROWS), 1)
            corner = jnp.where(key_ids <= row_ids, s[end - ROWS:], -1e30)
            s = corner if end == ROWS else jnp.concatenate([s[:end - ROWS], corner], axis=0)
            e = jnp.exp2((s - jnp.max(s, axis=0, keepdims=True)) * (FACTOR / math.log(2.0)))
            p = e * (1.0 / jnp.sum(e, axis=0, keepdims=True))
            gp = dot(v[:end], go, ((1,), (1,)))
            row_dot = jnp.sum(p * gp, axis=0, keepdims=True)
            gs = (p * (gp - row_dot) * FACTOR).astype(jnp.bfloat16)
            dv = dot(p.astype(jnp.bfloat16), go, ((1,), (0,)))
            dk = dot(gs, q, ((1,), (0,)))
            if block == half // ROWS - 1:
                v_acc[:end, :] = dv
                k_acc[:end, :] = dk
            else:
                v_acc[:end, :] += dv
                k_acc[:end, :] += dk
            dq = dot(k_turned[:, :end], gs, ((1,), (0,))).T
            dq_out[c, q_rows, lane] = dq.astype(jnp.bfloat16)
            sums_acc[head] += jnp.sum(dq.reshape(ROWS // 8, 8, HDIM), axis=0)
        dk_out[c, :total, lane] = k_acc[:total, :].astype(jnp.bfloat16)
        dv_out[c, :total, lane] = v_acc[:total, :].astype(jnp.bfloat16)

    results = (dq_out, dk_out, dv_out)
    finals = (dq_hbm, k_low, v_low)

    def rows_of(a, c, to):
        start = to * rows if a == 0 else (base + to) * rows
        return results[a].at[c, pl.ds(pl.multiple_of(start, rows), rows)]

    def send_results(c, chosen, first):
        item, part = c // parts, lax.rem(c, parts)

        def step(i, _):
            shift = (m - 1) - i // 2 - lax.rem(i, 2) * (m // 2)
            to = lax.rem(g + shift, m)
            climbs = jnp.logical_and(to >= m // 2, g < m // 2)

            if first:
                @pl.when(upper)
                def _():
                    for a, high in ((1, k_high), (2, v_high)):
                        remote(
                            results[a].at[c, pl.ds(pl.multiple_of(to * rows, rows), rows)],
                            high.at[item, :, column(g, part)],
                            high_send.at[c, a - 1], high_recv.at[c, a - 1], to,
                        )

            @pl.when(jnp.logical_and(shift > 0, chosen(climbs)))
            def _():
                for a in range(3):
                    remote(
                        rows_of(a, c, to), finals[a].at[item, :, column(g, part)],
                        out_send.at[c, a], out_recv.at[c, a], base + to,
                    )
            return 0

        lax.fori_loop(0, m, step, 0)

    def work(c, _):
        item, part = c // parts, lax.rem(c, parts)

        @pl.when(c + AHEAD < chunks)
        def _():
            send_inputs(c + AHEAD, 0)

        wait_bytes(q_in.at[c], in_recv.at[c, 0])
        wait_bytes(g_in.at[c], in_recv.at[c, 1])
        wait_bytes(k_in.at[c, :half], in_recv.at[c, 2])
        wait_bytes(v_in.at[c, :half], in_recv.at[c, 3])

        @pl.when(lower)
        def _():
            for h in range(chunk_heads):
                attend(c, part, h, 0)

        @pl.when(upper)
        def _():
            wait_bytes(k_in.at[c, :half], low_recv.at[c, 0])
            wait_bytes(v_in.at[c, :half], low_recv.at[c, 1])
            for h in range(chunk_heads):
                attend(c, part, h, half)

        last = chunks - 1
        send_results(c, lambda climbs: jnp.logical_or(jnp.logical_not(climbs), c == last), True)

        @pl.when(c == last - 1)
        def _():
            def release(held, _):
                send_results(held, lambda climbs: climbs, False)
                return 0

            lax.fori_loop(0, last, release, 0)

        for a in range(3):
            pltpu.make_async_copy(
                rows_of(a, c, g), finals[a].at[item, :, column(g, part)], out_recv.at[c, a]
            ).start()
        return 0

    lax.fori_loop(0, chunks, work, 0)

    if exchange:
        hand_out(
            owners, lambda j: sums_acc.at[j], sums_in.at[(me // m) * cores + core],
            sums_recv.at[0], sums_send,
        )

    def arrived(c, _):
        item, part = c // parts, lax.rem(c, parts)
        for a in range(3):
            wait_bytes(finals[a].at[0, :, pl.ds(0, m * cols)], out_recv.at[c, a])

        @pl.when(lower)
        def _():
            for a, high in ((0, k_high), (1, v_high)):
                wait_bytes(high.at[0, :, pl.ds(0, m * cols)], high_recv.at[c, a])

            def add(owner, _):
                lanes = column(owner, part)
                for low, high in ((k_low, k_high), (v_low, v_high)):
                    low[item, :, lanes] = (
                        low[item, :, lanes].astype(jnp.float32)
                        + high[item, :, lanes].astype(jnp.float32)
                    ).astype(jnp.bfloat16)
                return 0

            lax.fori_loop(0, m, add, 0)
        return 0

    lax.fori_loop(0, chunks, arrived, 0)

    ends = [
        pltpu.make_async_copy(low, out, last_sem.at[i])
        for i, (low, out) in enumerate(((k_low, dk_hbm), (v_low, dv_hbm)))
    ]
    for copy in ends:
        copy.start()

    def sent(c, _):
        less = (m - 1) * rows
        for a in range(4):
            wait_bytes(q_in.at[c, pl.ds(0, less)], in_send.at[c, a])
        for a in range(3):
            wait_bytes(dq_out.at[c, pl.ds(0, less)], out_send.at[c, a])

        @pl.when(lower)
        def _():
            for a in range(2):
                wait_bytes(q_in.at[c], low_send.at[c, a])

        @pl.when(upper)
        def _():
            for a in range(2):
                wait_bytes(dq_out.at[c], high_send.at[c, a])
        return 0

    lax.fori_loop(0, chunks, sent, 0)
    if exchange:
        wait_bytes(sums_in, sums_recv.at[0])
        sums_ref[...] = jnp.sum(jnp.sum(sums_in[...], axis=0), axis=0, keepdims=True)
        handed_out(workers, bias_in, bias_send)
        handed_out(owners, sums_acc, sums_send)
    else:
        sums_ref[...] = jnp.sum(sums_acc[...], axis=1)
    for copy in ends:
        copy.wait()


def body(n, cores, queries, key_states, value_states, grad_output, query_bias):
    items, rows, width = queries.shape
    m = n // 2
    heads = width // HDIM // m
    parts = min(4, heads)
    chunk_heads = heads // parts
    cols = chunk_heads * HDIM
    half = m * rows
    chunks = items * parts
    bf16, f32 = jnp.bfloat16, jnp.float32
    own = heads * HDIM
    group = lax.rem(lax.axis_index("seq"), m)

    exchange = width == HDIM * n * cores
    if exchange:
        bias = jnp.broadcast_to(query_bias.astype(f32)[None, :], (8, HDIM))
        sums_rows = 1
    else:
        whole_bias = lax.all_gather(query_bias, ("seq", "dp"), axis=0, tiled=True)
        bias = lax.dynamic_slice(whole_bias, (group * own,), (own,))
        bias = bias.astype(f32).reshape(heads, 1, HDIM)
        sums_rows = heads

    result = jax.ShapeDtypeStruct(queries.shape, bf16)
    dma = pltpu.SemaphoreType.DMA
    anywhere = pl.BlockSpec(memory_space=pl.ANY)
    local = pl.BlockSpec(memory_space=pltpu.VMEM)
    grad_queries, grad_keys, grad_values, sums = pl.pallas_call(
        functools.partial(kernel, n, cores, chunk_heads, parts, exchange),
        out_shape=(result, result, result, jax.ShapeDtypeStruct((sums_rows, HDIM), f32)),
        in_specs=[anywhere] * 4 + [local],
        out_specs=(anywhere, anywhere, anywhere, local),
        scratch_shapes=[
            pltpu.VMEM((chunks, half, cols), bf16),
            pltpu.VMEM((chunks, half, cols), bf16),
            pltpu.VMEM((chunks, 2 * half, cols), bf16),
            pltpu.VMEM((chunks, 2 * half, cols), bf16),
            pltpu.VMEM((chunks, half, cols), bf16),
            pltpu.VMEM((chunks, 2 * half, cols), bf16),
            pltpu.VMEM((chunks, 2 * half, cols), bf16),
            pltpu.VMEM(queries.shape, bf16),
            pltpu.VMEM(queries.shape, bf16),
            pltpu.VMEM(queries.shape, bf16),
            pltpu.VMEM(queries.shape, bf16),
            pltpu.VMEM((2 * half, HDIM), f32),
            pltpu.VMEM((2 * half, HDIM), f32),
            pltpu.VMEM((heads, 8, HDIM), f32),
            pltpu.VMEM((heads, 8, HDIM), f32),
            pltpu.VMEM((2 * cores, 8, HDIM), f32),
            dma((chunks, 4)), dma((chunks, 4)), dma((chunks, 2)), dma((chunks, 2)),
            dma((chunks, 3)), dma((chunks, 3)), dma((chunks, 2)), dma((chunks, 2)),
            dma((2,)), dma((1,)), dma((2 * cores,)), dma((1,)), dma((heads,)),
        ],
        compiler_params=pltpu.CompilerParams(
            collective_id=0, has_side_effects=True, vmem_limit_bytes=52 * 1024 * 1024
        ),
    )(queries, key_states, value_states, grad_output, bias)

    if exchange:
        return (grad_queries, grad_keys, grad_values, sums.reshape(HDIM))
    bias_total = lax.dynamic_update_slice(
        jnp.zeros((width,), f32), sums.reshape(own), (group * own,)
    )
    grad_bias = lax.psum_scatter(bias_total, ("seq", "dp"), scatter_dimension=0, tiled=True)
    return (grad_queries, grad_keys, grad_values, grad_bias)


def solution(mesh):
    in_specs = (
        P("dp", "seq", None),
        P("dp", "seq", None),
        P("dp", "seq", None),
        P("dp", "seq", None),
        P(("seq", "dp")),
    )
    out_specs = (P("dp", "seq", None), P("dp", "seq", None), P("dp", "seq", None), P(("seq", "dp")))
    return jax.shard_map(
        functools.partial(body, mesh.shape["seq"], mesh.shape["dp"]),
        mesh=mesh, in_specs=in_specs, out_specs=out_specs, check_vma=False,
    )
```

```python
import functools
import math

import jax
import jax.numpy as jnp
from jax import lax
from jax.experimental import pallas as pl
from jax.experimental.pallas import tpu as pltpu
from jax.sharding import PartitionSpec as P

HDIM = 128
ROWS = 256
FACTOR = 1.0 / math.sqrt(HDIM)
AHEAD = 3
MESH = pl.DeviceIdType.MESH


def dot(a, b, dims):
    return lax.dot_general(a, b, (dims, ((), ())), preferred_element_type=jnp.float32)


def wait_bytes(ref, sem):
    pltpu.make_async_copy(ref, ref, sem).wait()


def kernel(
    n, cores, chunk_heads, parts, exchange,
    q_hbm, k_hbm, v_hbm, g_hbm, bias_ref,
    dq_hbm, dk_hbm, dv_hbm, sums_ref,
    q_in, g_in, k_in, v_in,
    dq_out, dk_out, dv_out,
    k_low, v_low, k_high, v_high,
    k_acc, v_acc, bias_in, sums_acc, sums_in,
    in_recv, in_send, low_recv, low_send,
    out_recv, out_send, high_recv, high_send, last_sem,
    bias_recv, bias_send, sums_recv, sums_send,
):
    m = n // 2
    me = lax.axis_index("seq")
    upper = me >= m
    lower = me < m
    g = lax.rem(me, m)
    base = me - g
    items, rows, _ = q_hbm.shape
    half = m * rows
    cols = chunk_heads * HDIM
    own = parts * cols
    chunks = items * parts

    heads = parts * chunk_heads
    core = lax.axis_index("dp")
    flat = me * cores + core

    barrier = pltpu.get_barrier_semaphore()

    def greet(i, _):
        if exchange:
            other = lax.rem(flat + i, n * cores)
            target = {"seq": other // cores, "dp": lax.rem(other, cores)}
        else:
            target = {"seq": lax.rem(me + i, n)}
        pl.semaphore_signal(barrier, inc=1, device_id=target, device_id_type=MESH)
        return 0

    greeted = n * cores if exchange else n
    lax.fori_loop(1, greeted, greet, 0)
    pl.semaphore_wait(barrier, greeted - 1)

    owned = flat // heads
    workers = [(side * m + owned, dp) for side in range(2) for dp in range(cores)]
    owners = [
        ((g * heads + j) // cores, lax.rem(g * heads + j, cores)) for j in range(heads)
    ]

    def hand_out(targets, src_of, dst, recv, sends):
        for i, (seq, dp) in enumerate(targets):
            away = seq * cores + dp != flat

            @pl.when(away)
            def _():
                pltpu.make_async_remote_copy(
                    src_ref=src_of(i), dst_ref=dst, send_sem=sends.at[i], recv_sem=recv,
                    device_id={"seq": seq, "dp": dp}, device_id_type=MESH,
                ).start()

            @pl.when(jnp.logical_not(away))
            def _():
                pltpu.make_async_copy(src_of(i), dst, recv).start()

    def handed_out(targets, ref, sends):
        for i, (seq, dp) in enumerate(targets):
            @pl.when(seq * cores + dp != flat)
            def _():
                wait_bytes(ref.at[0], sends.at[i])

    if exchange:
        hand_out(
            workers, lambda i: bias_ref, bias_in.at[lax.rem(flat, heads)],
            bias_recv.at[0], bias_send,
        )

    def column(owner, part):
        return pl.ds(pl.multiple_of(owner * own + part * cols, 128), cols)

    def remote(src, dst, send, recv, peer):
        pltpu.make_async_remote_copy(
            src_ref=src, dst_ref=dst, send_sem=send, recv_sem=recv,
            device_id={"seq": peer}, device_id_type=MESH,
        ).start()

    sources = (q_hbm, g_hbm, k_hbm, v_hbm)
    landing = (q_in, g_in, k_in, v_in)

    def send_inputs(c, _):
        item, part = c // parts, lax.rem(c, parts)
        mine = pl.ds(pl.multiple_of(g * rows, rows), rows)
        at = pl.ds(pl.multiple_of(me * rows, rows), rows)

        def place(a):
            return landing[a].at[c, mine if a < 2 else at]

        def step(i, _):
            shift = (m - 1) - i // 2 - lax.rem(i, 2) * (m // 2)
            to = lax.rem(g + shift, m)

            @pl.when(lower)
            def _():
                for a in (2, 3):
                    remote(
                        sources[a].at[item, :, column(to, part)], landing[a].at[c, at],
                        low_send.at[c, a - 2], low_recv.at[c, a - 2], m + to,
                    )

            @pl.when(shift > 0)
            def _():
                for a in (2, 3, 0, 1):
                    remote(
                        sources[a].at[item, :, column(to, part)], place(a),
                        in_send.at[c, a], in_recv.at[c, a], base + to,
                    )
            return 0

        lax.fori_loop(0, m, step, 0)
        for a in range(4):
            pltpu.make_async_copy(
                sources[a].at[item, :, column(g, part)], place(a), in_recv.at[c, a]
            ).start()
        return 0

    lax.fori_loop(0, min(AHEAD, chunks), send_inputs, 0)
    sums_acc[...] = jnp.zeros_like(sums_acc)
    if exchange:
        wait_bytes(bias_in, bias_recv.at[0])

    def attend(c, part, h, offset):
        lane = pl.ds(h * HDIM, HDIM)
        total = offset + half
        k = k_in[c, :total, lane]
        v = v_in[c, :total, lane]
        k_turned = k.astype(jnp.float32).T.astype(jnp.bfloat16)
        head = part * chunk_heads + h
        bias = bias_in[head, :1, :] if exchange else bias_ref[head, :1, :]
        for block in reversed(range(half // ROWS)):
            q_rows = pl.ds(block * ROWS, ROWS)
            end = offset + (block + 1) * ROWS
            q = (q_in[c, q_rows, lane].astype(jnp.float32) + bias).astype(jnp.bfloat16)
            go = g_in[c, q_rows, lane]
            s = dot(k[:end], q, ((1,), (1,)))
            key_ids = lax.broadcasted_iota(jnp.int32, (ROWS, ROWS), 0)
            row_ids = lax.broadcasted_iota(jnp.int32, (ROWS, ROWS), 1)
            corner = jnp.where(key_ids <= row_ids, s[end - ROWS:], -1e30)
            s = corner if end == ROWS else jnp.concatenate([s[:end - ROWS], corner], axis=0)
            e = jnp.exp2((s - jnp.max(s, axis=0, keepdims=True)) * (FACTOR / math.log(2.0)))
            p = e * (1.0 / jnp.sum(e, axis=0, keepdims=True))
            gp = dot(v[:end], go, ((1,), (1,)))
            row_dot = jnp.sum(p * gp, axis=0, keepdims=True)
            gs = (p * (gp - row_dot) * FACTOR).astype(jnp.bfloat16)
            dv = dot(p.astype(jnp.bfloat16), go, ((1,), (0,)))
            dk = dot(gs, q, ((1,), (0,)))
            if block == half // ROWS - 1:
                v_acc[:end, :] = dv
                k_acc[:end, :] = dk
            else:
                v_acc[:end, :] += dv
                k_acc[:end, :] += dk
            dq = dot(k_turned[:, :end], gs, ((1,), (0,))).T
            dq_out[c, q_rows, lane] = dq.astype(jnp.bfloat16)
            sums_acc[head] += jnp.sum(dq.reshape(ROWS // 8, 8, HDIM), axis=0)
        dk_out[c, :total, lane] = k_acc[:total, :].astype(jnp.bfloat16)
        dv_out[c, :total, lane] = v_acc[:total, :].astype(jnp.bfloat16)

    results = (dq_out, dk_out, dv_out)
    finals = (dq_hbm, k_low, v_low)

    def rows_of(a, c, to):
        start = to * rows if a == 0 else (base + to) * rows
        return results[a].at[c, pl.ds(pl.multiple_of(start, rows), rows)]

    def send_results(c):
        item, part = c // parts, lax.rem(c, parts)

        def step(i, _):
            shift = (m - 1) - i // 2 - lax.rem(i, 2) * (m // 2)
            to = lax.rem(g + shift, m)

            @pl.when(upper)
            def _():
                for a, high in ((1, k_high), (2, v_high)):
                    remote(
                        results[a].at[c, pl.ds(pl.multiple_of(to * rows, rows), rows)],
                        high.at[item, :, column(g, part)],
                        high_send.at[c, a - 1], high_recv.at[c, a - 1], to,
                    )

            @pl.when(shift > 0)
            def _():
                for a in range(3):
                    remote(
                        rows_of(a, c, to), finals[a].at[item, :, column(g, part)],
                        out_send.at[c, a], out_recv.at[c, a], base + to,
                    )
            return 0

        lax.fori_loop(0, m, step, 0)

    def work(c, _):
        item, part = c // parts, lax.rem(c, parts)

        @pl.when(c + AHEAD < chunks)
        def _():
            send_inputs(c + AHEAD, 0)

        wait_bytes(q_in.at[c], in_recv.at[c, 0])
        wait_bytes(g_in.at[c], in_recv.at[c, 1])
        wait_bytes(k_in.at[c, :half], in_recv.at[c, 2])
        wait_bytes(v_in.at[c, :half], in_recv.at[c, 3])

        @pl.when(lower)
        def _():
            for h in range(chunk_heads):
                attend(c, part, h, 0)

        @pl.when(upper)
        def _():
            wait_bytes(k_in.at[c, :half], low_recv.at[c, 0])
            wait_bytes(v_in.at[c, :half], low_recv.at[c, 1])
            for h in range(chunk_heads):
                attend(c, part, h, half)

        send_results(c)

        for a in range(3):
            pltpu.make_async_copy(
                rows_of(a, c, g), finals[a].at[item, :, column(g, part)], out_recv.at[c, a]
            ).start()
        return 0

    lax.fori_loop(0, chunks, work, 0)

    if exchange:
        hand_out(
            owners, lambda j: sums_acc.at[j], sums_in.at[(me // m) * cores + core],
            sums_recv.at[0], sums_send,
        )

    def arrived(c, _):
        item, part = c // parts, lax.rem(c, parts)
        for a in range(3):
            wait_bytes(finals[a].at[0, :, pl.ds(0, m * cols)], out_recv.at[c, a])

        @pl.when(lower)
        def _():
            for a, high in ((0, k_high), (1, v_high)):
                wait_bytes(high.at[0, :, pl.ds(0, m * cols)], high_recv.at[c, a])

            def add(owner, _):
                lanes = column(owner, part)
                for low, high in ((k_low, k_high), (v_low, v_high)):
                    low[item, :, lanes] = (
                        low[item, :, lanes].astype(jnp.float32)
                        + high[item, :, lanes].astype(jnp.float32)
                    ).astype(jnp.bfloat16)
                return 0

            lax.fori_loop(0, m, add, 0)
        return 0

    lax.fori_loop(0, chunks, arrived, 0)

    ends = [
        pltpu.make_async_copy(low, out, last_sem.at[i])
        for i, (low, out) in enumerate(((k_low, dk_hbm), (v_low, dv_hbm)))
    ]
    for copy in ends:
        copy.start()

    def sent(c, _):
        less = (m - 1) * rows
        for a in range(4):
            wait_bytes(q_in.at[c, pl.ds(0, less)], in_send.at[c, a])
        for a in range(3):
            wait_bytes(dq_out.at[c, pl.ds(0, less)], out_send.at[c, a])

        @pl.when(lower)
        def _():
            for a in range(2):
                wait_bytes(q_in.at[c], low_send.at[c, a])

        @pl.when(upper)
        def _():
            for a in range(2):
                wait_bytes(dq_out.at[c], high_send.at[c, a])
        return 0

    lax.fori_loop(0, chunks, sent, 0)
    if exchange:
        wait_bytes(sums_in, sums_recv.at[0])
        sums_ref[...] = jnp.sum(jnp.sum(sums_in[...], axis=0), axis=0, keepdims=True)
        handed_out(workers, bias_in, bias_send)
        handed_out(owners, sums_acc, sums_send)
    else:
        sums_ref[...] = jnp.sum(sums_acc[...], axis=1)
    for copy in ends:
        copy.wait()


def body(n, cores, queries, key_states, value_states, grad_output, query_bias):
    items, rows, width = queries.shape
    m = n // 2
    heads = width // HDIM // m
    parts = min(4, heads)
    chunk_heads = heads // parts
    cols = chunk_heads * HDIM
    half = m * rows
    chunks = items * parts
    bf16, f32 = jnp.bfloat16, jnp.float32
    own = heads * HDIM
    group = lax.rem(lax.axis_index("seq"), m)

    exchange = width == HDIM * n * cores
    if exchange:
        bias = jnp.broadcast_to(query_bias.astype(f32)[None, :], (8, HDIM))
        sums_rows = 1
    else:
        whole_bias = lax.all_gather(query_bias, ("seq", "dp"), axis=0, tiled=True)
        bias = lax.dynamic_slice(whole_bias, (group * own,), (own,))
        bias = bias.astype(f32).reshape(heads, 1, HDIM)
        sums_rows = heads

    result = jax.ShapeDtypeStruct(queries.shape, bf16)
    dma = pltpu.SemaphoreType.DMA
    anywhere = pl.BlockSpec(memory_space=pl.ANY)
    local = pl.BlockSpec(memory_space=pltpu.VMEM)
    grad_queries, grad_keys, grad_values, sums = pl.pallas_call(
        functools.partial(kernel, n, cores, chunk_heads, parts, exchange),
        out_shape=(result, result, result, jax.ShapeDtypeStruct((sums_rows, HDIM), f32)),
        in_specs=[anywhere] * 4 + [local],
        out_specs=(anywhere, anywhere, anywhere, local),
        scratch_shapes=[
            pltpu.VMEM((chunks, half, cols), bf16),
            pltpu.VMEM((chunks, half, cols), bf16),
            pltpu.VMEM((chunks, 2 * half, cols), bf16),
            pltpu.VMEM((chunks, 2 * half, cols), bf16),
            pltpu.VMEM((chunks, half, cols), bf16),
            pltpu.VMEM((chunks, 2 * half, cols), bf16),
            pltpu.VMEM((chunks, 2 * half, cols), bf16),
            pltpu.VMEM(queries.shape, bf16),
            pltpu.VMEM(queries.shape, bf16),
            pltpu.VMEM(queries.shape, bf16),
            pltpu.VMEM(queries.shape, bf16),
            pltpu.VMEM((2 * half, HDIM), f32),
            pltpu.VMEM((2 * half, HDIM), f32),
            pltpu.VMEM((heads, 8, HDIM), f32),
            pltpu.VMEM((heads, 8, HDIM), f32),
            pltpu.VMEM((2 * cores, 8, HDIM), f32),
            dma((chunks, 4)), dma((chunks, 4)), dma((chunks, 2)), dma((chunks, 2)),
            dma((chunks, 3)), dma((chunks, 3)), dma((chunks, 2)), dma((chunks, 2)),
            dma((2,)), dma((1,)), dma((2 * cores,)), dma((1,)), dma((heads,)),
        ],
        compiler_params=pltpu.CompilerParams(
            collective_id=0, has_side_effects=True, vmem_limit_bytes=52 * 1024 * 1024
        ),
    )(queries, key_states, value_states, grad_output, bias)

    if exchange:
        return (grad_queries, grad_keys, grad_values, sums.reshape(HDIM))
    bias_total = lax.dynamic_update_slice(
        jnp.zeros((width,), f32), sums.reshape(own), (group * own,)
    )
    grad_bias = lax.psum_scatter(bias_total, ("seq", "dp"), scatter_dimension=0, tiled=True)
    return (grad_queries, grad_keys, grad_values, grad_bias)


def solution(mesh):
    in_specs = (
        P("dp", "seq", None),
        P("dp", "seq", None),
        P("dp", "seq", None),
        P("dp", "seq", None),
        P(("seq", "dp")),
    )
    out_specs = (P("dp", "seq", None), P("dp", "seq", None), P("dp", "seq", None), P(("seq", "dp")))
    return jax.shard_map(
        functools.partial(body, mesh.shape["seq"], mesh.shape["dp"]),
        mesh=mesh, in_specs=in_specs, out_specs=out_specs, check_vma=False,
    )
```
